32 devices in a mesh: row: 8 (over z, x), col: 4 (over y, core).
Axes of the slice: x: 2, y: 2, z: 4, core: 2. Of those that a mesh axis runs over, the one named last changes fastest.
Arguments:
- queries: bfloat16 [16, 768, 768], P('row', 'col'), may hold values from -18 to 18
- keys: bfloat16 [16, 768, 768], P('col', 'row'), may hold values from -18 to 18
Outputs:
- grad_queries: float32 [16, 768, 768], P('row', 'col')
- grad_keys: float32 [16, 768, 768], P('col', 'row')
The draws below stay inside these ranges and needn't reach their ends.
All inputs are finite; a program needn't handle non-finite values.
Results may differ from the reference program's by a relative error of at most 0.005.
Values may be sent and summed in bfloat16 or wider, within the bound.
No kernel may reach another device: no remote copies, remote signals or barrier semaphores. Data moves between devices by JAX's collectives and lax.ppermute only.
A program may use at most 128 MiB of HBM per device.

```python
import jax
import jax.numpy as jnp
from jax import lax

D = 768
FRAMES = 16
TOK = 768


def make_view(key, salt):
    base = jax.random.fold_in(key, 7)
    scene_key = jax.random.fold_in(base, 1)
    noise_key = jax.random.fold_in(jax.random.fold_in(base, 11), salt)
    scene = jnp.clip(jax.random.normal(scene_key, (TOK, D), jnp.float32), -4.0, 4.0)
    noise = jnp.clip(jax.random.normal(noise_key, (FRAMES, TOK, D), jnp.float32), -4.0, 4.0)
    view = 0.5 * scene[None] + 0.87 * noise
    return view.astype(jnp.bfloat16)


def draw_queries(key, part):
    return make_view(key, 0)


def draw_keys(key, part):
    return make_view(key, 1)


def setup_inputs(seed: int = 0) -> dict:
    streams_of = jax.random.split(jax.random.key(seed), 3)
    queries = draw_queries(jax.random.fold_in(streams_of[2], 71), 0)
    keys = draw_keys(jax.random.fold_in(streams_of[2], 71), 0)
    return dict(queries=queries, keys=keys)


def contract(left_side, right_side, left_dim, right_dim):
    return lax.dot_general(left_side, right_side, (((left_dim,), (right_dim,)), ((), ())), preferred_element_type=jnp.float32)


def cycle_terms(query_frame, key_frame, score_scale, frames):
    scores = score_scale * contract(query_frame, key_frame, 1, 1)
    by_rows = jax.nn.softmax(scores, axis=1)
    by_cols = jax.nn.softmax(scores, axis=0)
    rows_half = by_rows.astype(jnp.bfloat16)
    cols_half = by_cols.astype(jnp.bfloat16)
    warped = contract(cols_half, query_frame, 0, 0).astype(jnp.bfloat16)
    cycled = jnp.dot(rows_half, warped, preferred_element_type=jnp.float32)
    residual = (cycled - query_frame.astype(jnp.float32)) / frames
    resid_half = residual.astype(jnp.bfloat16)
    grad_rows = contract(resid_half, warped, 1, 1)
    grad_warp = contract(rows_half, resid_half, 0, 0).astype(jnp.bfloat16)
    grad_cols = contract(query_frame, grad_warp, 1, 1)
    grad_scores = by_rows * (grad_rows - jnp.sum(grad_rows * by_rows, axis=1, keepdims=True))
    grad_scores = grad_scores + by_cols * (grad_cols - jnp.sum(grad_cols * by_cols, axis=0, keepdims=True))
    score_half = (score_scale * grad_scores).astype(jnp.bfloat16)
    return cols_half, grad_warp, score_half, residual


def reference(queries, keys):
    frames = queries.shape[0]
    score_scale = queries.shape[2] ** -0.5

    def add_pair(pair_index, totals):
        grad_q, grad_k = totals
        source_at = pair_index // frames
        target_at = pair_index % frames
        query_frame = lax.dynamic_index_in_dim(queries, source_at, 0, False)
        key_frame = lax.dynamic_index_in_dim(keys, target_at, 0, False)
        cols_half, grad_warp, score_half, residual = cycle_terms(query_frame, key_frame, score_scale, frames)
        q_term = jnp.dot(cols_half, grad_warp, preferred_element_type=jnp.float32)
        q_term = q_term + jnp.dot(score_half, key_frame, preferred_element_type=jnp.float32) - residual
        k_term = contract(score_half, query_frame, 0, 0)
        return grad_q.at[source_at].add(q_term), grad_k.at[target_at].add(k_term)

    empty_q = jnp.zeros(queries.shape, jnp.float32)
    empty_k = jnp.zeros(keys.shape, jnp.float32)
    grad_q, grad_k = lax.fori_loop(0, frames * frames, add_pair, (empty_q, empty_k))
    return grad_q, grad_k
```

```python
import functools
import math

import jax
import jax.numpy as jnp
from jax import lax
from jax.experimental import pallas as pl
from jax.experimental.pallas import tpu as pltpu
from jax.sharding import PartitionSpec as P

F32 = jnp.float32
BF16 = jnp.bfloat16
OFFSET = 2.0


def nt(left, right):
    return lax.dot_general(left, right, (((1,), (1,)), ((), ())), preferred_element_type=F32)


def nn(left, right):
    return lax.dot_general(left, right, (((1,), (0,)), ((), ())), preferred_element_type=F32)


def tile_of(size, most):
    for tile in range(most, 0, -128):
        if size % tile == 0:
            return tile
    return size


def fold(value, how):
    rows, width = value.shape
    return how(value.reshape(rows // 8, 8, width), axis=0)


def pair_steps(at, first, frames, scale, q_ref, qt_ref, k_ref, acc_ref, ktt_ref, wait_acc, done_acc, scratch):
    (s_ref, a_ref, ah_ref, eh_ref, vt_ref, gh_ref, ght_ref, dvt_ref, dvs_ref, db_ref, da_ref, dsh_ref) = [
        ref.at[at] for ref in scratch
    ]
    q_ref, qt_ref, acc_ref = q_ref.at[at], qt_ref.at[at], acc_ref.at[at]
    tokens = q_ref.shape[0]
    keys = k_ref.shape[0]
    width = q_ref.shape[1]
    tile, ktile, dtile = tile_of(tokens, 256), tile_of(keys, 256), tile_of(width, 256)
    chunk = 32 if tile % 32 == 0 else 8
    rows = [slice(o, o + tile) for o in range(0, tokens, tile)]
    cols = [slice(o, o + ktile) for o in range(0, keys, ktile)]
    feats = [slice(o, o + dtile) for o in range(0, width, dtile)]

    def chunks(of):
        return [slice(o, o + chunk) for o in range(of.start, of.stop, chunk)]

    to_log2 = scale * math.log2(math.e)
    todo = []

    def some(count, work):
        for part in todo[:count]:
            work(part)
        del todo[:count]

    colmax = []

    def by_rows(part):
        t = s_ref[part, :]
        e = jnp.exp2(t - jnp.max(t, axis=1, keepdims=True))
        a = e * (1.0 / jnp.sum(e, axis=1, keepdims=True))
        a_ref[part, :] = a
        ah_ref[part, :] = a.astype(BF16)
        top = fold(t, jnp.max)
        colmax[:] = [jnp.maximum(colmax[0], top) if colmax else top]

    per = -(-tile // chunk // len(cols))
    for rb in rows:
        for cb in cols:
            s_ref[rb, cb] = nt(q_ref[rb, :], k_ref[cb, :]) * to_log2
            some(per, by_rows)
            yield 0.1
        todo += chunks(rb)
    while todo:
        some(1, by_rows)
        yield 0.03
    colmax = jnp.max(colmax[0], axis=0, keepdims=True)

    colsum = 0.0
    for part in chunks(slice(0, tokens)):
        e = jnp.exp2(s_ref[part, :] - colmax)
        s_ref[part, :] = e
        eh_ref[part, :] = e.astype(BF16)
        colsum = colsum + fold(e, jnp.sum)
        yield 0.02
    inv = 1.0 / jnp.sum(colsum, axis=0, keepdims=True)

    for fb in feats:
        for cb in cols:
            vt_ref[fb, cb] = (nn(qt_ref[fb, :], eh_ref[:, cb]) * inv[:, cb]).astype(BF16)
            yield 0.1
    wait_acc(at)
    for rb in rows:
        for fb in feats:
            g = (nt(ah_ref[rb, :], vt_ref[fb, :]) - q_ref[rb, fb].astype(F32)) * (1.0 / frames)
            gh = g.astype(BF16)
            gh_ref[rb, fb] = gh
            ght_ref[fb, rb] = gh.T
            acc_ref[rb, fb] = -g if first else acc_ref[rb, fb] - g
            yield 0.1
    for fb in feats:
        for cb in cols:
            dv = nn(ght_ref[fb, :], ah_ref[:, cb])
            dvt_ref[fb, cb] = dv.astype(BF16)
            dvs_ref[fb, cb] = (dv * inv[:, cb]).astype(BF16)
            yield 0.1
    colcor = [0.0] * len(cols)
    for rb in rows:
        for n, cb in enumerate(cols):
            db = nn(q_ref[rb, :], dvt_ref[:, cb])
            db_ref[rb, cb] = db
            colcor[n] = colcor[n] + fold(db * s_ref[rb, cb], jnp.sum)
            yield 0.1
    colcor = jnp.concatenate([jnp.sum(c, axis=0, keepdims=True) for c in colcor], axis=1) * inv

    def score_grad(part):
        da = da_ref[part, :]
        a = a_ref[part, :]
        rowcor = jnp.sum(da * a, axis=1, keepdims=True)
        ds = a * (da - rowcor) + s_ref[part, :] * ((db_ref[part, :] - colcor) * inv)
        dsh_ref[part, :] = (ds * scale).astype(BF16)

    for rb in rows:
        for cb in cols:
            da_ref[rb, cb] = nn(gh_ref[rb, :], vt_ref[:, cb])
            some(per, score_grad)
            yield 0.1
        todo += chunks(rb)
    for rb in rows:
        for fb in feats:
            acc_ref[rb, fb] += nt(eh_ref[rb, :], dvs_ref[fb, :])
            some(per, score_grad)
            yield 0.1
    some(len(todo), score_grad)
    for rb in rows:
        for fb in feats:
            acc_ref[rb, fb] += nn(dsh_ref[rb, :], k_ref[:, fb])
            yield 0.1
    done_acc(at)
    for fb in feats:
        for cb in cols:
            kt = nn(qt_ref[fb, :], dsh_ref[:, cb])
            ktt_ref[fb, cb] = kt if at == 0 else ktt_ref[fb, cb] + kt
            yield 0.1


def interleave(streams, offset):
    clocks = [n * offset for n in range(len(streams))]
    while streams:
        n = min(range(len(streams)), key=lambda at: clocks[at])
        try:
            clocks[n] += next(streams[n])
        except StopIteration:
            del streams[n], clocks[n]


def pairs_kernel(frames, scale, hi, relative, first, last, n_q, n_k, *refs):
    refs = list(refs)

    def take(count):
        got = refs[:count]
        del refs[:count]
        return got

    (me_ref,) = take(1)
    q_blocks, k_blocks = take(n_q), take(n_k)
    acc_in = None if first else take(1)[0]
    if last:
        q_send, q_keep = take(2)
    else:
        (acc_out,) = take(1)
    k_send, k_keep = take(2)
    q_ref, qt_ref, k_ref, acc_ref, ktt_ref, kt_ref = take(6)
    if last:
        (qh_ref,) = take(1)
    (sems,) = take(1)
    scratch = refs
    sources, tokens, width = q_ref.shape
    keys = k_ref.shape[0]
    copy = pltpu.make_async_copy
    used = [0]

    def sem():
        used[0] += 1
        return sems.at[used[0] - 1]

    loads = []
    size = keys // n_k
    for n, block in enumerate(k_blocks):
        loads.append(copy(block, k_ref.at[pl.ds(n * size, size)], sem()))
    size = tokens // n_q
    for n, block in enumerate(q_blocks):
        for at in range(sources):
            loads.append(copy(block.at[at], q_ref.at[at, pl.ds(n * size, size)], sem()))
    acc_loads = [] if first else [copy(acc_in.at[at], acc_ref.at[at], sem()) for at in range(sources)]
    for load in loads + acc_loads:
        load.start()
    for load in loads:
        load.wait()
    tile = tile_of(tokens, 256)
    for at in range(sources):
        for o in range(0, tokens, tile):
            qt_ref[at, :, o : o + tile] = q_ref[at, o : o + tile, :].T
    stores = []

    def wait_acc(at):
        if not first:
            acc_loads[at].wait()

    def done_acc(at):
        if last:
            qh_ref[at] = acc_ref[at].astype(BF16)
            for m in range(n_q):
                part = pl.ds(m * size, size)
                if m % 2:
                    stores.append(copy(qh_ref.at[at, part], q_send.at[m // 2, at], sem()))
                else:
                    stores.append(copy(acc_ref.at[at, part], q_keep.at[m // 2, at], sem()))
                stores[-1].start()
        else:
            stores.append(copy(acc_ref.at[at], acc_out.at[at], sem()))
            stores[-1].start()

    interleave(
        [
            pair_steps(at, first, frames, scale, q_ref, qt_ref, k_ref, acc_ref, ktt_ref, wait_acc, done_acc, scratch)
            for at in range(sources)
        ],
        OFFSET,
    )
    tile = tile_of(width, 256)
    for o in range(0, width, tile):
        kt_ref[:, o : o + tile] = ktt_ref[o : o + tile, :].astype(BF16).T
    count = 2 * hi
    size = keys // count
    for m in range(count):
        here = m if relative else me_ref[0] ^ m
        start = pl.multiple_of(here * size, size)
        to = k_send if m % 2 else k_keep
        stores.append(copy(kt_ref.at[pl.ds(start, size)], to.at[m // 2], sem()))
        stores[-1].start()
    for store in stores:
        store.wait()


def pairs_call(me, q_blocks, k_blocks, acc, frames, hi, relative, last):
    first = acc is None
    sources, size, width = q_blocks[0].shape
    tokens = size * len(q_blocks)
    keys = sum(block.shape[0] for block in k_blocks)
    anywhere = pl.BlockSpec(memory_space=pl.ANY)
    in_vmem = pltpu.VMEM
    inputs = [me, *q_blocks, *k_blocks] + ([] if first else [acc])
    k_out = [jax.ShapeDtypeStruct((hi, keys // (2 * hi), width), BF16)] * 2
    half = len(q_blocks) // 2
    if last:
        q_out = [
            jax.ShapeDtypeStruct((half, sources, size, width), BF16),
            jax.ShapeDtypeStruct((half, sources, size, width), F32),
        ]
    else:
        q_out = [jax.ShapeDtypeStruct((sources, tokens, width), F32)]
    copies = len(k_blocks) + sources * (2 * len(q_blocks) + 2) + 2 * hi + 4
    scratch = [
        in_vmem((sources, tokens, width), BF16),
        in_vmem((sources, width, tokens), BF16),
        in_vmem((keys, width), BF16),
        in_vmem((sources, tokens, width), F32),
        in_vmem((width, keys), F32),
        in_vmem((keys, width), BF16),
    ]
    if last:
        scratch.append(in_vmem((sources, tokens, width), BF16))
    scratch.append(pltpu.SemaphoreType.DMA((copies,)))
    full = lambda r, c, t: in_vmem((sources, r, c), t)
    scratch += [
        full(tokens, keys, F32),
        full(tokens, keys, F32),
        full(tokens, keys, BF16),
        full(tokens, keys, BF16),
        full(width, keys, BF16),
        full(tokens, width, BF16),
        full(width, tokens, BF16),
        full(width, keys, BF16),
        full(width, keys, BF16),
        full(tokens, keys, F32),
        full(tokens, keys, F32),
        full(tokens, keys, BF16),
    ]
    flops = 18 * sources * tokens * keys * width
    return pl.pallas_call(
        functools.partial(
            pairs_kernel, frames, width**-0.5, hi, relative, first, last, len(q_blocks), len(k_blocks)
        ),
        in_specs=[pl.BlockSpec(memory_space=pltpu.SMEM)] + [anywhere] * (len(inputs) - 1),
        out_specs=[anywhere] * (len(q_out) + 2),
        out_shape=q_out + k_out,
        scratch_shapes=scratch,
        input_output_aliases={} if first or last else {len(inputs) - 1: 0},
        compiler_params=pltpu.CompilerParams(vmem_limit_bytes=62 * 2**20),
        cost_estimate=pl.CostEstimate(
            flops=flops, bytes_accessed=sources * tokens * width * 12, transcendentals=2 * sources * tokens * keys
        ),
        name="pairs",
    )(*inputs)


def local(queries, keys):
    n_row, n_col = lax.axis_size("row"), lax.axis_size("col")
    row_hi, col_hi = n_row // 2, n_col // 2
    sources, targets = queries.shape[0], keys.shape[0]
    frames = sources * n_row

    def swap(value, axis, offset):
        count = lax.axis_size(axis)
        return lax.ppermute(value, axis, [(at, at ^ offset) for at in range(count)])

    def gather(own, axis, hi):
        far = [own] + [swap(own, axis, 2 * k) for k in range(1, hi)]
        near = [swap(block, axis, 1) for block in far]
        return [block for both in zip(far, near) for block in both]

    me = lax.axis_index("row").astype(jnp.int32).reshape(1)
    q_blocks = gather(queries, "col", col_hi)
    k_first = gather(keys[0], "row", row_hi)
    acc = None
    k_parts = []
    for target in range(targets):
        last = target == targets - 1
        if target == 0:
            k_blocks = k_first
        else:
            k_blocks = [lax.all_gather(keys[target], "row", axis=0, tiled=True)]
        out = pairs_call(me, q_blocks, k_blocks, acc, frames, row_hi, target == 0, last)
        acc = out[0]
        k_parts.append((out[-2], out[-1]))

    def scatter(send, keep, axis, hi):
        both = keep.astype(F32) + swap(send, axis, 1).astype(F32)
        total = both[0]
        for k in range(1, hi):
            total = total + swap(both[k].astype(BF16), axis, 2 * k).astype(F32)
        return total

    out_k = jnp.stack([scatter(send, keep, "row", row_hi) for send, keep in k_parts])
    out_q = scatter(out[0], out[1], "col", col_hi)
    return (out_q, out_k)


def solution(mesh):
    placed = (P("row", "col", None), P("col", "row", None))
    return jax.shard_map(local, mesh=mesh, in_specs=placed, out_specs=placed, check_vma=False)
```

```python
import functools
import math

import jax
import jax.numpy as jnp
from jax import lax
from jax.experimental import pallas as pl
from jax.experimental.pallas import tpu as pltpu
from jax.sharding import PartitionSpec as P

F32 = jnp.float32
BF16 = jnp.bfloat16
OFFSET = 0.0


def nt(left, right):
    return lax.dot_general(left, right, (((1,), (1,)), ((), ())), preferred_element_type=F32)


def nn(left, right):
    return lax.dot_general(left, right, (((1,), (0,)), ((), ())), preferred_element_type=F32)


def tile_of(size, most):
    for tile in range(most, 0, -128):
        if size % tile == 0:
            return tile
    return size


def fold(value, how):
    rows, width = value.shape
    return how(value.reshape(rows // 8, 8, width), axis=0)


def pair_steps(at, first, frames, scale, q_ref, qt_ref, k_ref, acc_ref, ktt_ref, hooks, scratch):
    (s_ref, a_ref, ah_ref, eh_ref, vt_ref, gh_ref, ght_ref, dvt_ref, dvs_ref, db_ref, da_ref, dsh_ref) = [
        ref.at[at] for ref in scratch
    ]
    q_ref, qt_ref, acc_ref = q_ref.at[at], qt_ref.at[at], acc_ref.at[at]
    wait_acc, done_acc = hooks
    tokens = q_ref.shape[0]
    keys = k_ref.shape[0]
    width = q_ref.shape[1]
    tile, ktile, dtile = tile_of(tokens, 256), tile_of(keys, 256), tile_of(width, 256)
    chunk = 32 if tile % 32 == 0 else 8
    rows = [slice(o, o + tile) for o in range(0, tokens, tile)]
    cols = [slice(o, o + ktile) for o in range(0, keys, ktile)]
    feats = [slice(o, o + dtile) for o in range(0, width, dtile)]

    def chunks(of):
        return [slice(o, o + chunk) for o in range(of.start, of.stop, chunk)]

    to_log2 = scale * math.log2(math.e)
    todo = []

    def some(count, work):
        for part in todo[:count]:
            work(part)
        del todo[:count]

    colmax = []

    def by_rows(part):
        t = s_ref[part, :]
        e = jnp.exp2(t - jnp.max(t, axis=1, keepdims=True))
        a = e * (1.0 / jnp.sum(e, axis=1, keepdims=True))
        a_ref[part, :] = a
        ah_ref[part, :] = a.astype(BF16)
        top = fold(t, jnp.max)
        colmax[:] = [jnp.maximum(colmax[0], top) if colmax else top]

    per = -(-tile // chunk // len(cols))
    for rb in rows:
        for cb in cols:
            s_ref[rb, cb] = nt(q_ref[rb, :], k_ref[cb, :]) * to_log2
            some(per, by_rows)
            yield 0.1
        todo += chunks(rb)
    while todo:
        some(1, by_rows)
        yield 0.03
    colmax = jnp.max(colmax[0], axis=0, keepdims=True)

    for rb in rows:
        qt_ref[:, rb] = q_ref[rb, :].T

    colsum = 0.0
    for part in chunks(slice(0, tokens)):
        e = jnp.exp2(s_ref[part, :] - colmax)
        s_ref[part, :] = e
        eh_ref[part, :] = e.astype(BF16)
        colsum = colsum + fold(e, jnp.sum)
        yield 0.02
    inv = 1.0 / jnp.sum(colsum, axis=0, keepdims=True)

    for fb in feats:
        for cb in cols:
            vt_ref[fb, cb] = (nn(qt_ref[fb, :], eh_ref[:, cb]) * inv[:, cb]).astype(BF16)
            yield 0.1
    wait_acc(at)
    for rb in rows:
        for fb in feats:
            g = (nt(ah_ref[rb, :], vt_ref[fb, :]) - q_ref[rb, fb].astype(F32)) * (1.0 / frames)
            gh = g.astype(BF16)
            gh_ref[rb, fb] = gh
            ght_ref[fb, rb] = gh.T
            acc_ref[rb, fb] = -g if first else acc_ref[rb, fb] - g
            yield 0.1
    for fb in feats:
        for cb in cols:
            dv = nn(ght_ref[fb, :], ah_ref[:, cb])
            dvt_ref[fb, cb] = dv.astype(BF16)
            dvs_ref[fb, cb] = (dv * inv[:, cb]).astype(BF16)
            yield 0.1
    colcor = [0.0] * len(cols)
    for rb in rows:
        for n, cb in enumerate(cols):
            db = nn(q_ref[rb, :], dvt_ref[:, cb])
            db_ref[rb, cb] = db
            colcor[n] = colcor[n] + fold(db * s_ref[rb, cb], jnp.sum)
            yield 0.1
    colcor = jnp.concatenate([jnp.sum(c, axis=0, keepdims=True) for c in colcor], axis=1) * inv

    def score_grad(part):
        da = da_ref[part, :]
        a = a_ref[part, :]
        rowcor = jnp.sum(da * a, axis=1, keepdims=True)
        ds = a * (da - rowcor) + s_ref[part, :] * ((db_ref[part, :] - colcor) * inv)
        dsh_ref[part, :] = (ds * scale).astype(BF16)

    for rb in rows:
        for cb in cols:
            da_ref[rb, cb] = nn(gh_ref[rb, :], vt_ref[:, cb])
            some(per, score_grad)
            yield 0.1
        todo += chunks(rb)
    for rb in rows:
        for fb in feats:
            acc_ref[rb, fb] += nt(eh_ref[rb, :], dvs_ref[fb, :])
            some(per, score_grad)
            yield 0.1
    some(len(todo), score_grad)
    for rb in rows:
        for fb in feats:
            acc_ref[rb, fb] += nn(dsh_ref[rb, :], k_ref[:, fb])
            yield 0.1
    done_acc(at)
    for fb in feats:
        for cb in cols:
            kt = nn(qt_ref[fb, :], dsh_ref[:, cb])
            ktt_ref[fb, cb] = kt if at == 0 else ktt_ref[fb, cb] + kt
            yield 0.1


def interleave(streams, offset):
    clocks = [n * offset for n in range(len(streams))]
    while streams:
        n = min(range(len(streams)), key=lambda at: clocks[at])
        try:
            clocks[n] += next(streams[n])
        except StopIteration:
            del streams[n], clocks[n]


def pairs_kernel(frames, scale, hi, first, last, n_q, k_slots, slot, *refs):
    refs = list(refs)

    def take(count):
        got = refs[:count]
        del refs[:count]
        return got

    n_k = len(k_slots)
    q_blocks, k_blocks = take(n_q), take(n_k)
    acc_in = None if first else take(1)[0]
    if slot:
        take(2)
    if last:
        q_send, q_keep = take(2)
    else:
        (acc_out,) = take(1)
    k_send, k_keep = (take(2), take(1)[0]) if last else take(2)
    q_ref, qt_ref, k_ref, acc_ref, ktt_ref, kt_ref = take(6)
    if last:
        (qh_ref,) = take(1)
    (sems,) = take(1)
    scratch = refs
    sources, tokens, width = q_ref.shape
    keys = k_ref.shape[0]
    copy = pltpu.make_async_copy
    used = [0]

    def sem():
        used[0] += 1
        return sems.at[used[0] - 1]

    k_size, size = keys // n_k, tokens // n_q
    k_loads = [copy(block.at[k_slots[n]], k_ref.at[pl.ds(n * k_size, k_size)], sem()) for n, block in enumerate(k_blocks)]
    q_loads = [
        [copy(block.at[at], q_ref.at[at, pl.ds(n * size, size)], sem()) for n, block in enumerate(q_blocks)]
        for at in range(sources)
    ]
    acc_loads = [] if first else [copy(acc_in.at[at], acc_ref.at[at], sem()) for at in range(sources)]
    for load in q_loads[0] + k_loads + sum(q_loads[1:], []) + acc_loads:
        load.start()

    for load in q_loads[0] + k_loads + sum(q_loads[1:], []):
        load.wait()
    stores = []

    def wait_acc(at):
        if not first:
            acc_loads[at].wait()

    def done_acc(at):
        if last:
            qh_ref[at] = acc_ref[at].astype(BF16)
            for m in range(n_q):
                part = pl.ds(m * size, size)
                if m % 2:
                    stores.append(copy(qh_ref.at[at, part], q_send.at[m // 2, at], sem()))
                else:
                    stores.append(copy(acc_ref.at[at, part], q_keep.at[m // 2, at], sem()))
                stores[-1].start()
        else:
            stores.append(copy(acc_ref.at[at], acc_out.at[at], sem()))
            stores[-1].start()

    hooks = wait_acc, done_acc
    interleave(
        [
            pair_steps(at, first, frames, scale, q_ref, qt_ref, k_ref, acc_ref, ktt_ref, hooks, scratch)
            for at in range(sources)
        ],
        OFFSET,
    )
    tile = tile_of(width, 256)
    for o in range(0, width, tile):
        kt_ref[:, o : o + tile] = ktt_ref[o : o + tile, :].astype(BF16).T
    count = 2 * hi
    k_part = keys // count
    for m in range(count):
        to = k_send if m % 2 else k_keep
        at = m // 2
        if last and m % 2:
            to = k_send[0] if at >= hi // 2 else k_send[1]
            at = at % (hi // 2)
        stores.append(copy(kt_ref.at[pl.ds(m * k_part, k_part)], to.at[at, slot], sem()))
        stores[-1].start()
    for store in stores:
        store.wait()


def pairs_call(q_blocks, k_blocks, acc, parts, frames, hi, slots, slot, last):
    first = acc is None
    sources, size, width = q_blocks[0].shape
    tokens = size * len(q_blocks)
    keys = sum(block.shape[1] for block, _ in k_blocks)
    anywhere = pl.BlockSpec(memory_space=pl.ANY)
    in_vmem = pltpu.VMEM
    inputs = [*q_blocks, *[block for block, _ in k_blocks]] + ([] if first else [acc]) + (list(parts) if slot else [])
    k_out = [jax.ShapeDtypeStruct((hi, slots, keys // (2 * hi), width), BF16)] * 2
    if last:
        few = jax.ShapeDtypeStruct((hi // 2, *k_out[0].shape[1:]), BF16)
        k_out = [few, few, k_out[1]]
    half = len(q_blocks) // 2
    if last:
        q_out = [
            jax.ShapeDtypeStruct((half, sources, size, width), BF16),
            jax.ShapeDtypeStruct((half, sources, size, width), F32),
        ]
    else:
        q_out = [jax.ShapeDtypeStruct((sources, tokens, width), F32)]
    copies = len(k_blocks) + sources * (2 * len(q_blocks) + 2) + 2 * hi
    scratch = [
        in_vmem((sources, tokens, width), BF16),
        in_vmem((sources, width, tokens), BF16),
        in_vmem((keys, width), BF16),
        in_vmem((sources, tokens, width), F32),
        in_vmem((width, keys), F32),
        in_vmem((keys, width), BF16),
    ]
    if last:
        scratch.append(in_vmem((sources, tokens, width), BF16))
    scratch.append(pltpu.SemaphoreType.DMA((copies,)))
    full = lambda r, c, t: in_vmem((sources, r, c), t)
    scratch += [
        full(tokens, keys, F32),
        full(tokens, keys, F32),
        full(tokens, keys, BF16),
        full(tokens, keys, BF16),
        full(width, keys, BF16),
        full(tokens, width, BF16),
        full(width, tokens, BF16),
        full(width, keys, BF16),
        full(width, keys, BF16),
        full(tokens, keys, F32),
        full(tokens, keys, F32),
        full(tokens, keys, BF16),
    ]
    aliases = {} if first or last else {len(q_blocks) + len(k_blocks): 0}
    if slot:
        aliases.update({len(inputs) - 2: len(q_out), len(inputs) - 1: len(q_out) + 1})
    flops = 18 * sources * tokens * keys * width
    outs = pl.pallas_call(
        functools.partial(
            pairs_kernel, frames, width**-0.5, hi, first, last, len(q_blocks), [at for _, at in k_blocks], slot
        ),
        in_specs=[anywhere] * len(inputs),
        out_specs=[anywhere] * (len(q_out) + len(k_out)),
        out_shape=q_out + k_out,
        scratch_shapes=scratch,
        input_output_aliases=aliases,
        compiler_params=pltpu.CompilerParams(vmem_limit_bytes=62 * 2**20),
        cost_estimate=pl.CostEstimate(
            flops=flops, bytes_accessed=sources * tokens * width * 12, transcendentals=2 * sources * tokens * keys
        ),
        name="pairs",
    )(*inputs)
    return (tuple(outs[:2]) if last else outs[0]), tuple(outs[len(q_out):])


def local(queries, keys):
    n_row, n_col = lax.axis_size("row"), lax.axis_size("col")
    row_hi, col_hi = n_row // 2, n_col // 2
    sources, targets = queries.shape[0], keys.shape[0]
    frames = sources * n_row
    in_groups = [g for g in (range(0, 1), range(1, min(2, targets)), range(2, targets)) if len(g)]
    out_groups = [range(0, min(2, targets - 1))] + [range(t, t + 1) for t in range(2, targets)]
    out_groups = [g for g in out_groups if len(g)] if targets > 2 else [range(t, t + 1) for t in range(targets)]

    def swap(value, axis, offset):
        count = lax.axis_size(axis)
        return lax.ppermute(value, axis, [(at, at ^ offset) for at in range(count)])

    def far_of(own, axis, hi):
        return [swap(own, axis, 2 * k) for k in range(1, hi)]

    def near_of(far, axis):
        return [swap(block, axis, 1) for block in far]

    have = dict(queries=queries, keys=keys)
    last_out = len(out_groups) - 1
    for stage in range(-2, targets):
        new = {}
        for n, group in enumerate(in_groups):
            own = have["keys"][group.start : group.stop]
            if n == stage + 2:
                new["far", n] = far_of(own, "row", row_hi)
            if n == 0 and stage == -2:
                new["near_own", 0] = swap(own, "row", 1)
            if n == stage + 1:
                new["near", n] = near_of(have["far", n], "row")
        if stage == 0 and targets > 1:
            new["near_own", 1] = swap(have["keys"][1:], "row", 1)
        if stage == -2:
            new["far_q"] = far_of(have["queries"], "col", col_hi)
            new["near_own_q"] = swap(have["queries"], "col", 1)
        if stage == -1:
            new["near_q"] = near_of(have["far_q"], "col")
        for n, group in enumerate(out_groups):
            if stage == group.stop and stage < targets:
                send, keep = have["parts", n]
                new["half", n] = swap(send, "row", 1), keep
            if stage == group.stop + 1 and stage < targets:
                got, keep = have["half", n]
                both = keep.astype(F32) + got.astype(F32)
                new["sums", n] = [both[0]] + [swap(both[k].astype(BF16), "row", 2 * k) for k in range(1, row_hi)]
        if 0 <= stage < targets:
            n = min(stage, 2)
            slot = stage - in_groups[n].start
            k_blocks = [(have["keys"], stage)]
            k_blocks.append((have["near_own", min(stage, 1)], max(stage - 1, 0)))
            for far, near in zip(have["far", n], have["near", n]):
                k_blocks += [(far, slot), (near, slot)]
            q_blocks = [have["queries"], have["near_own_q"]]
            for far, near in zip(have["far_q"], have["near_q"]):
                q_blocks += [far, near]
            (m,) = [m for m, g in enumerate(out_groups) if stage in g]
            group = out_groups[m]
            new["acc"], new["parts", m] = pairs_call(
                q_blocks, k_blocks, have.get("acc"), have.get(("parts", m)), frames, row_hi,
                len(group), stage - group.start, stage == targets - 1,
            )
        have.update(new)
        names = list(have)
        have = dict(zip(names, lax.optimization_barrier(tuple(have[name] for name in names))))

    far_send, near_send, keep = have["parts", last_out]
    cut = row_hi // 2
    half = [keep[k].astype(F32) for k in range(row_hi)]
    got = swap(far_send, "row", 1)
    send_q, keep_q = have["acc"]
    got_q = swap(send_q, "col", 1)
    for n, group in enumerate(out_groups[:-1]):
        if group.stop == targets - 1:
            sent, kept = have["half", n]
            both = kept.astype(F32) + sent.astype(F32)
            have["sums", n] = [both[0]] + [swap(both[k].astype(BF16), "row", 2 * k) for k in range(1, row_hi)]
    got, got_q, near_send = lax.optimization_barrier((got, got_q, near_send))
    half_q = keep_q + got_q.astype(F32)
    upper = [swap((half[k] + got[k - cut].astype(F32)).astype(BF16), "row", 2 * k) for k in range(cut, row_hi)]
    got = swap(near_send, "row", 1)
    sums_q = [half_q[0]] + [swap(half_q[k].astype(BF16), "col", 2 * k) for k in range(1, col_hi)]
    lower = [half[k] + got[k].astype(F32) for k in range(cut)]
    have["sums", last_out] = lower[:1] + [swap(lower[k].astype(BF16), "row", 2 * k) for k in range(1, cut)] + upper

    def add_up(parts):
        total = parts[0]
        for part in parts[1:]:
            total = total + part.astype(F32)
        return total

    out_k = jnp.concatenate([add_up(have["sums", n]) for n in range(len(out_groups))])
    return (add_up(sums_q), out_k)


def solution(mesh):
    placed = (P("row", "col", None), P("col", "row", None))
    return jax.shard_map(local, mesh=mesh, in_specs=placed, out_specs=placed, check_vma=False)
```

```python
import functools
import math

import jax
import jax.numpy as jnp
from jax import lax
from jax.experimental import pallas as pl
from jax.experimental.pallas import tpu as pltpu
from jax.sharding import PartitionSpec as P

F32 = jnp.float32
BF16 = jnp.bfloat16
OFFSET = 0.0


def nt(left, right):
    return lax.dot_general(left, right, (((1,), (1,)), ((), ())), preferred_element_type=F32)


def nn(left, right):
    return lax.dot_general(left, right, (((1,), (0,)), ((), ())), preferred_element_type=F32)


def tile_of(size, most):
    for tile in range(most, 0, -128):
        if size % tile == 0:
            return tile
    return size


def fold(value, how):
    rows, width = value.shape
    return how(value.reshape(rows // 8, 8, width), axis=0)


def pair_steps(at, first, frames, scale, q_ref, qt_ref, k_ref, acc_ref, ktt_ref, hooks, scratch):
    (s_ref, a_ref, ah_ref, eh_ref, vt_ref, gh_ref, ght_ref, dvt_ref, dvs_ref, db_ref, da_ref, dsh_ref) = [
        ref.at[at] for ref in scratch
    ]
    q_ref, qt_ref, acc_ref = q_ref.at[at], qt_ref.at[at], acc_ref.at[at]
    wait_acc, done_acc = hooks
    tokens = q_ref.shape[0]
    keys = k_ref.shape[0]
    width = q_ref.shape[1]
    tile, ktile, dtile = tile_of(tokens, 256), tile_of(keys, 256), tile_of(width, 256)
    chunk = 16 if tile % 16 == 0 else 8
    rows = [slice(o, o + tile) for o in range(0, tokens, tile)]
    cols = [slice(o, o + ktile) for o in range(0, keys, ktile)]
    feats = [slice(o, o + dtile) for o in range(0, width, dtile)]

    def chunks(of):
        return [slice(o, o + chunk) for o in range(of.start, of.stop, chunk)]

    to_log2 = scale * math.log2(math.e)
    todo = []

    def some(count, work):
        for part in todo[:count]:
            work(part)
        del todo[:count]

    colmax = []

    def by_rows(part):
        t = s_ref[part, :]
        e = jnp.exp2(t - jnp.max(t, axis=1, keepdims=True))
        a = e * (1.0 / jnp.sum(e, axis=1, keepdims=True))
        a_ref[part, :] = a
        ah_ref[part, :] = a.astype(BF16)
        top = fold(t, jnp.max)
        colmax[:] = [jnp.maximum(colmax[0], top) if colmax else top]

    per = -(-tile // chunk // len(cols))
    for rb in rows:
        for cb in cols:
            s_ref[rb, cb] = nt(q_ref[rb, :], k_ref[cb, :]) * to_log2
            some(per, by_rows)
            yield 0.1
        todo += chunks(rb)
    while todo:
        some(1, by_rows)
        yield 0.03
    colmax = jnp.max(colmax[0], axis=0, keepdims=True)

    for rb in rows:
        qt_ref[:, rb] = q_ref[rb, :].T

    colsum = 0.0
    for part in chunks(slice(0, tokens)):
        e = jnp.exp2(s_ref[part, :] - colmax)
        s_ref[part, :] = e
        eh_ref[part, :] = e.astype(BF16)
        colsum = colsum + fold(e, jnp.sum)
        yield 0.02
    inv = 1.0 / jnp.sum(colsum, axis=0, keepdims=True)

    for fb in feats:
        for cb in cols:
            vt_ref[fb, cb] = (nn(qt_ref[fb, :], eh_ref[:, cb]) * inv[:, cb]).astype(BF16)
            yield 0.1
    wait_acc(at)
    for rb in rows:
        for fb in feats:
            g = (nt(ah_ref[rb, :], vt_ref[fb, :]) - q_ref[rb, fb].astype(F32)) * (1.0 / frames)
            gh = g.astype(BF16)
            gh_ref[rb, fb] = gh
            ght_ref[fb, rb] = gh.T
            acc_ref[rb, fb] = -g if first else acc_ref[rb, fb] - g
            yield 0.1
    for fb in feats:
        for cb in cols:
            dv = nn(ght_ref[fb, :], ah_ref[:, cb])
            dvt_ref[fb, cb] = dv.astype(BF16)
            dvs_ref[fb, cb] = (dv * inv[:, cb]).astype(BF16)
            yield 0.1
    colcor = [0.0] * len(cols)
    for rb in rows:
        for n, cb in enumerate(cols):
            db = nn(q_ref[rb, :], dvt_ref[:, cb])
            db_ref[rb, cb] = db
            colcor[n] = colcor[n] + fold(db * s_ref[rb, cb], jnp.sum)
            yield 0.1
    colcor = jnp.concatenate([jnp.sum(c, axis=0, keepdims=True) for c in colcor], axis=1) * inv

    def score_grad(part):
        da = da_ref[part, :]
        a = a_ref[part, :]
        rowcor = jnp.sum(da * a, axis=1, keepdims=True)
        ds = a * (da - rowcor) + s_ref[part, :] * ((db_ref[part, :] - colcor) * inv)
        dsh_ref[part, :] = (ds * scale).astype(BF16)

    for rb in rows:
        for cb in cols:
            da_ref[rb, cb] = nn(gh_ref[rb, :], vt_ref[:, cb])
            some(per, score_grad)
            yield 0.1
        todo += chunks(rb)
    for rb in rows:
        for fb in feats:
            acc_ref[rb, fb] += nt(eh_ref[rb, :], dvs_ref[fb, :])
            some(per, score_grad)
            yield 0.1
    some(len(todo), score_grad)
    for rb in rows:
        for fb in feats:
            acc_ref[rb, fb] += nn(dsh_ref[rb, :], k_ref[:, fb])
            yield 0.1
    done_acc(at)
    for fb in feats:
        for cb in cols:
            kt = nn(qt_ref[fb, :], dsh_ref[:, cb])
            ktt_ref[fb, cb] = kt if at == 0 else ktt_ref[fb, cb] + kt
            yield 0.1


def interleave(streams, offset):
    clocks = [n * offset for n in range(len(streams))]
    while streams:
        n = min(range(len(streams)), key=lambda at: clocks[at])
        try:
            clocks[n] += next(streams[n])
        except StopIteration:
            del streams[n], clocks[n]


def pairs_kernel(frames, scale, hi, first, last, n_q, k_slots, slot, *refs):
    refs = list(refs)

    def take(count):
        got = refs[:count]
        del refs[:count]
        return got

    n_k = len(k_slots)
    q_blocks, k_blocks = take(n_q), take(n_k)
    acc_in = None if first else take(1)[0]
    if slot:
        take(2)
    if last:
        q_send, q_keep = take(2)
    else:
        (acc_out,) = take(1)
    k_send, k_keep = (take(2), take(1)[0]) if last else take(2)
    q_ref, qt_ref, k_ref, acc_ref, ktt_ref, kt_ref = take(6)
    if last:
        (qh_ref,) = take(1)
    (sems,) = take(1)
    scratch = refs
    sources, tokens, width = q_ref.shape
    keys = k_ref.shape[0]
    copy = pltpu.make_async_copy
    used = [0]

    def sem():
        used[0] += 1
        return sems.at[used[0] - 1]

    k_size, size = keys // n_k, tokens // n_q
    k_loads = [copy(block.at[k_slots[n]], k_ref.at[pl.ds(n * k_size, k_size)], sem()) for n, block in enumerate(k_blocks)]
    q_loads = [
        [copy(block.at[at], q_ref.at[at, pl.ds(n * size, size)], sem()) for n, block in enumerate(q_blocks)]
        for at in range(sources)
    ]
    acc_loads = [] if first else [copy(acc_in.at[at], acc_ref.at[at], sem()) for at in range(sources)]
    for load in q_loads[0] + k_loads + sum(q_loads[1:], []) + acc_loads:
        load.start()

    for load in q_loads[0] + k_loads + sum(q_loads[1:], []):
        load.wait()
    stores = []

    def wait_acc(at):
        if not first:
            acc_loads[at].wait()

    def done_acc(at):
        if last:
            qh_ref[at] = acc_ref[at].astype(BF16)
            for m in range(n_q):
                part = pl.ds(m * size, size)
                if m % 2:
                    stores.append(copy(qh_ref.at[at, part], q_send.at[m // 2, at], sem()))
                else:
                    stores.append(copy(acc_ref.at[at, part], q_keep.at[m // 2, at], sem()))
                stores[-1].start()
        else:
            stores.append(copy(acc_ref.at[at], acc_out.at[at], sem()))
            stores[-1].start()

    hooks = wait_acc, done_acc
    interleave(
        [
            pair_steps(at, first, frames, scale, q_ref, qt_ref, k_ref, acc_ref, ktt_ref, hooks, scratch)
            for at in range(sources)
        ],
        OFFSET,
    )
    tile = tile_of(width, 256)
    for o in range(0, width, tile):
        kt_ref[:, o : o + tile] = ktt_ref[o : o + tile, :].astype(BF16).T
    count = 2 * hi
    k_part = keys // count
    for m in range(count):
        to = k_send if m % 2 else k_keep
        at = m // 2
        if last and m % 2:
            to = k_send[0] if at >= hi // 2 else k_send[1]
            at = at % (hi // 2)
        stores.append(copy(kt_ref.at[pl.ds(m * k_part, k_part)], to.at[at, slot], sem()))
        stores[-1].start()
    for store in stores:
        store.wait()


def pairs_call(q_blocks, k_blocks, acc, parts, frames, hi, slots, slot, last):
    first = acc is None
    sources, size, width = q_blocks[0].shape
    tokens = size * len(q_blocks)
    keys = sum(block.shape[1] for block, _ in k_blocks)
    anywhere = pl.BlockSpec(memory_space=pl.ANY)
    in_vmem = pltpu.VMEM
    inputs = [*q_blocks, *[block for block, _ in k_blocks]] + ([] if first else [acc]) + (list(parts) if slot else [])
    k_out = [jax.ShapeDtypeStruct((hi, slots, keys // (2 * hi), width), BF16)] * 2
    if last:
        few = jax.ShapeDtypeStruct((hi // 2, *k_out[0].shape[1:]), BF16)
        k_out = [few, few, k_out[1]]
    half = len(q_blocks) // 2
    if last:
        q_out = [
            jax.ShapeDtypeStruct((half, sources, size, width), BF16),
            jax.ShapeDtypeStruct((half, sources, size, width), F32),
        ]
    else:
        q_out = [jax.ShapeDtypeStruct((sources, tokens, width), F32)]
    copies = len(k_blocks) + sources * (2 * len(q_blocks) + 2) + 2 * hi
    scratch = [
        in_vmem((sources, tokens, width), BF16),
        in_vmem((sources, width, tokens), BF16),
        in_vmem((keys, width), BF16),
        in_vmem((sources, tokens, width), F32),
        in_vmem((width, keys), F32),
        in_vmem((keys, width), BF16),
    ]
    if last:
        scratch.append(in_vmem((sources, tokens, width), BF16))
    scratch.append(pltpu.SemaphoreType.DMA((copies,)))
    full = lambda r, c, t: in_vmem((sources, r, c), t)
    scratch += [
        full(tokens, keys, F32),
        full(tokens, keys, F32),
        full(tokens, keys, BF16),
        full(tokens, keys, BF16),
        full(width, keys, BF16),
        full(tokens, width, BF16),
        full(width, tokens, BF16),
        full(width, keys, BF16),
        full(width, keys, BF16),
        full(tokens, keys, F32),
        full(tokens, keys, F32),
        full(tokens, keys, BF16),
    ]
    aliases = {} if first or last else {len(q_blocks) + len(k_blocks): 0}
    if slot:
        aliases.update({len(inputs) - 2: len(q_out), len(inputs) - 1: len(q_out) + 1})
    flops = 18 * sources * tokens * keys * width
    outs = pl.pallas_call(
        functools.partial(
            pairs_kernel, frames, width**-0.5, hi, first, last, len(q_blocks), [at for _, at in k_blocks], slot
        ),
        in_specs=[anywhere] * len(inputs),
        out_specs=[anywhere] * (len(q_out) + len(k_out)),
        out_shape=q_out + k_out,
        scratch_shapes=scratch,
        input_output_aliases=aliases,
        compiler_params=pltpu.CompilerParams(vmem_limit_bytes=62 * 2**20),
        cost_estimate=pl.CostEstimate(
            flops=flops, bytes_accessed=sources * tokens * width * 12, transcendentals=2 * sources * tokens * keys
        ),
        name="pairs",
    )(*inputs)
    return (tuple(outs[:2]) if last else outs[0]), tuple(outs[len(q_out):])


def local(queries, keys):
    n_row, n_col = lax.axis_size("row"), lax.axis_size("col")
    row_hi, col_hi = n_row // 2, n_col // 2
    sources, targets = queries.shape[0], keys.shape[0]
    frames = sources * n_row
    in_groups = [g for g in (range(0, 1), range(1, min(2, targets)), range(2, targets)) if len(g)]
    out_groups = [range(0, min(2, targets - 1))] + [range(t, t + 1) for t in range(2, targets)]
    out_groups = [g for g in out_groups if len(g)] if targets > 2 else [range(t, t + 1) for t in range(targets)]

    def swap(value, axis, offset):
        count = lax.axis_size(axis)
        return lax.ppermute(value, axis, [(at, at ^ offset) for at in range(count)])

    def far_of(own, axis, hi):
        return [swap(own, axis, 2 * k) for k in range(1, hi)]

    def near_of(far, axis):
        return [swap(block, axis, 1) for block in far]

    def row_sums(keep, got):
        both = [keep[k].astype(F32) + got[k].astype(F32) for k in range(row_hi)]
        return both[:1] + [swap(both[k].astype(BF16), "row", 2 * k) for k in range(1, row_hi)]

    have = dict(queries=queries, keys=keys)
    last_out = len(out_groups) - 1
    for stage in range(-2, targets):
        new = {}
        if stage == -1:
            new["near_own_q"] = swap(have["queries"], "col", 1)
            new["near_q"] = near_of(have["far_q"], "col")
        for n, group in enumerate(in_groups):
            own = have["keys"][group.start : group.stop]
            if n == stage + 2:
                if stage == -1:
                    own = lax.optimization_barrier((own, new["near_own_q"]))[0]
                new["far", n] = far_of(own, "row", row_hi)
            if n == stage + 1:
                new["near", n] = near_of(have["far", n], "row")
        if stage == -2:
            new["near_own"] = swap(have["keys"], "row", 1)
            new["far_q"] = far_of(have["queries"], "col", col_hi)
        for n, group in enumerate(out_groups):
            if stage == group.stop and stage < targets:
                send, keep = have["parts", n]
                new["half", n] = swap(send, "row", 1), keep
            if stage == group.stop + 1 and stage < targets:
                got, keep = have["half", n]
                new["sums", n] = row_sums(keep, got)
        if 0 <= stage < targets:
            n = min(stage, 2)
            slot = stage - in_groups[n].start
            k_blocks = [(have["keys"], stage), (have["near_own"], stage)]
            for far, near in zip(have["far", n], have["near", n]):
                k_blocks += [(far, slot), (near, slot)]
            q_blocks = [have["queries"], have["near_own_q"]]
            for far, near in zip(have["far_q"], have["near_q"]):
                q_blocks += [far, near]
            (m,) = [m for m, g in enumerate(out_groups) if stage in g]
            group = out_groups[m]
            new["acc"], new["parts", m] = pairs_call(
                q_blocks, k_blocks, have.get("acc"), have.get(("parts", m)), frames, row_hi,
                len(group), stage - group.start, stage == targets - 1,
            )
        have.update(new)
        names = list(have)
        have = dict(zip(names, lax.optimization_barrier(tuple(have[name] for name in names))))

    far_send, near_send, keep = have["parts", last_out]
    cut = row_hi // 2
    half = [keep[k].astype(F32) for k in range(row_hi)]
    got = swap(far_send, "row", 1)
    send_q, keep_q = have["acc"]
    got_q = swap(send_q, "col", 1)
    for n, group in enumerate(out_groups[:-1]):
        if group.stop == targets - 1:
            sent, kept = have["half", n]
            have["sums", n] = row_sums(kept, sent)
    got, got_q, near_send = lax.optimization_barrier((got, got_q, near_send))
    half_q = [keep_q[k] + got_q[k].astype(F32) for k in range(col_hi)]
    upper = [swap((half[k] + got[k - cut].astype(F32)).astype(BF16), "row", 2 * k) for k in range(cut, row_hi)]
    got = swap(near_send, "row", 1)
    sums_q = [half_q[0]] + [swap(half_q[k].astype(BF16), "col", 2 * k) for k in range(1, col_hi)]
    lower = [half[k] + got[k].astype(F32) for k in range(cut)]
    have["sums", last_out] = lower[:1] + [swap(lower[k].astype(BF16), "row", 2 * k) for k in range(1, cut)] + upper

    def add_up(parts):
        total = parts[0]
        for part in parts[1:]:
            total = total + part.astype(F32)
        return total

    out_k = jnp.concatenate([add_up(have["sums", n]) for n in range(len(out_groups))])
    return (add_up(sums_q), out_k)


def solution(mesh):
    placed = (P("row", "col", None), P("col", "row", None))
    return jax.shard_map(local, mesh=mesh, in_specs=placed, out_specs=placed, check_vma=False)
```
